256 devices in a mesh: blk: 64 (over z_hi, y, x, core), group: 4 (over z_lo).
Axes of the slice: x: 4, y: 4, z: 8 (z_hi: 2, z_lo: 4; z = z_hi * 4 + z_lo), core: 2. Of those that a mesh axis runs over, the one named last changes fastest.
Arguments:
- visual_encoder_outputs: float32 [131072, 1152], P(('blk', 'group'))
- caption_encoder_outputs: float32 [131072, 1152], P(('blk', 'group'))
- partner_lookup_grid: int32 [2, 64], replicated, may hold values from 0 to 63, as said below
- sharpness_coefficient: float32 [1], replicated, may hold values from 8 to 30
- sigmoid_shift_term: float32 [1], replicated, may hold values from -6 to -2
Outputs:
- image_gradient: float32 [131072, 1152], P(('blk', 'group'))
- text_gradient: float32 [131072, 1152], P(('blk', 'group'))
The draws below stay inside these ranges and needn't reach their ends.
Inputs may be any that keep to these rules, and one draw needn't show every extreme that they name: In each of the 2 rounds, partner_lookup_grid pairs index b of blk with index b XOR 2**k, where k is a bit position drawn for that round; the rounds' positions differ, so every matching is mutual and no index meets the same partner twice.
All inputs are finite; a program needn't handle non-finite values.
Results may differ from the reference program's by a relative error of at most 0.0049.
Values may be sent and summed in bfloat16 or wider, within the bound.
A program may use at most 64 MiB of HBM per device.

```python
import math
import jax
import jax.numpy as jnp
from jax import lax

D = 1152
ROWS = 512
ROUNDS = 2
PEERS = 64
BATCH = 131072
N_BLK = 64
N_GROUP = 4


def shared_rows(key):
    return jax.random.normal(key, (BATCH, D), jnp.float32)


def embedding_rows(key, common):
    private_key, scale_key = jax.random.split(key, 2)
    private = jax.random.normal(private_key, (BATCH, D), jnp.float32)
    row_scale = jnp.exp(jax.random.uniform(scale_key, (BATCH, 1), jnp.float32, math.log(0.2), math.log(2.0)))
    return (0.6 * common + 0.8 * private) * row_scale * D ** (-0.5)


def draw_visual_encoder_outputs(key, part):
    common = shared_rows(key)
    key = jax.random.fold_in(key, 21)
    return embedding_rows(key, common)


def draw_caption_encoder_outputs(key, part):
    common = shared_rows(key)
    key = jax.random.fold_in(key, 22)
    return embedding_rows(key, common)


def draw_partner_lookup_grid(key, part):
    key = jax.random.fold_in(key, 23)
    bit_total = PEERS.bit_length() - 1
    positions = jax.random.permutation(key, bit_total)[:ROUNDS].astype(jnp.int32)
    round_masks = jnp.left_shift(jnp.ones_like(positions), positions).astype(jnp.int32)
    indices = jnp.arange(PEERS, dtype=jnp.int32)
    return jnp.bitwise_xor(indices[None, :], round_masks[:, None]).astype(jnp.int32)


def setup_inputs(seed: int = 0) -> dict:
    key_of = jax.random.split(jax.random.key(seed), 6)
    return {
        "visual_encoder_outputs": draw_visual_encoder_outputs(jax.random.fold_in(key_of[5], 71), 0),
        "caption_encoder_outputs": draw_caption_encoder_outputs(jax.random.fold_in(key_of[5], 71), 0),
        "partner_lookup_grid": draw_partner_lookup_grid(jax.random.fold_in(key_of[5], 71), 0),
        "sharpness_coefficient": jnp.clip(jnp.exp(jax.random.uniform(key_of[3], (1,), jnp.float32, math.log(8.0), math.log(30.0))), 8.0, 30.0),
        "sigmoid_shift_term": jnp.clip(jax.random.uniform(key_of[4], (1,), jnp.float32, -6.0, -2.0), -6.0, -2.0),
    }


epsilon = 1e-06

def normalize(raw_rows):
    radius = jnp.sqrt(lax.optimization_barrier(jnp.sum(raw_rows * raw_rows, axis=-1, keepdims=True)) + epsilon)
    unit_rows = raw_rows / radius
    return (radius, unit_rows, unit_rows.astype(jnp.bfloat16))

def pair_linkage(left_rows, right_rows, similarity_multiplier, offset_value, matched):
    products = lax.dot_general(left_rows, right_rows, (((1,), (1,)), ((), ())), preferred_element_type=jnp.float32)
    logits = similarity_multiplier * products + offset_value
    if matched:
        labels = 2.0 * jnp.eye(left_rows.shape[0], dtype=jnp.float32) - 1.0
    else:
        labels = -jnp.ones_like(logits)
    weights = -labels * jax.nn.sigmoid(-labels * logits)
    return (similarity_multiplier * weights).astype(jnp.bfloat16)

def toward_left(coupled, right_rows):
    return jnp.dot(coupled, right_rows, preferred_element_type=jnp.float32)

def toward_right(coupled, left_rows):
    return lax.dot_general(coupled, left_rows, (((0,), (0,)), ((), ())), preferred_element_type=jnp.float32)

def rounded_term(values):
    return lax.optimization_barrier(values.astype(jnp.bfloat16)).astype(jnp.float32)

def project(radius, unit_rows, gradient):
    radial = lax.optimization_barrier(jnp.sum(unit_rows * gradient, axis=-1, keepdims=True))
    return (gradient - unit_rows * radial) / radius

def reference(visual_encoder_outputs, caption_encoder_outputs, partner_lookup_grid, sharpness_coefficient, sigmoid_shift_term):
    similarity_multiplier = sharpness_coefficient[0]
    offset_value = sigmoid_shift_term[0]
    image_raw = visual_encoder_outputs.reshape(N_BLK, N_GROUP, ROWS, D)
    text_raw = caption_encoder_outputs.reshape(N_BLK, N_GROUP, ROWS, D)
    image_split_pieces = normalize(image_raw)[2]
    text_halves = normalize(text_raw)[2]

    def per_accelerator_share(device_index):
        block_index = device_index // N_GROUP
        group_index = device_index % N_GROUP
        prior_group = (group_index + N_GROUP - 1) % N_GROUP
        next_group = (group_index + 1) % N_GROUP
        own_image = image_split_pieces[block_index, group_index]
        own_text = text_halves[block_index, group_index]
        diagonal = pair_linkage(own_image, own_text, similarity_multiplier, offset_value, True)
        image_sum = toward_left(diagonal, own_text)
        text_sum = toward_right(diagonal, own_image)
        prior_text = text_halves[block_index, prior_group]
        image_sum = image_sum + toward_left(pair_linkage(own_image, prior_text, similarity_multiplier, offset_value, False), prior_text)
        next_image = image_split_pieces[block_index, next_group]
        text_sum = text_sum + rounded_term(toward_right(pair_linkage(next_image, own_text, similarity_multiplier, offset_value, False), next_image))
        for number in range(ROUNDS):
            partner_block = partner_lookup_grid[number, block_index]
            other_text = text_halves[partner_block, group_index]
            other_image = image_split_pieces[partner_block, group_index]
            image_sum = image_sum + toward_left(pair_linkage(own_image, other_text, similarity_multiplier, offset_value, False), other_text)
            text_sum = text_sum + rounded_term(toward_right(pair_linkage(other_image, own_text, similarity_multiplier, offset_value, False), other_image))
        image_parts = normalize(image_raw[block_index, group_index])
        text_parts = normalize(text_raw[block_index, group_index])
        return (project(image_parts[0], image_parts[1], image_sum), project(text_parts[0], text_parts[1], text_sum))
    image_gradient, text_gradient = lax.map(per_accelerator_share, jnp.arange(N_BLK * N_GROUP, dtype=jnp.int32))
    return (image_gradient.reshape(BATCH, D), text_gradient.reshape(BATCH, D))
```

```python
import functools

import jax
import jax.numpy as jnp
from jax import lax
from jax.experimental import pallas as pl
from jax.experimental.pallas import tpu as pltpu
from jax.sharding import PartitionSpec as P

MESH = pl.DeviceIdType.MESH
epsilon = 1e-06
CHUNKS = 8


def flipped(bits):
    mask = sum(1 << bit for bit in bits)
    return (mask, 0)


def there(move, blk, group, groups):
    mask, step = move
    return (jnp.bitwise_xor(blk, mask), lax.rem(group + step + groups, groups))


def plan(bits):
    transfers = [((0, 1), 0), ((0, -1), 1)]
    low, high = bits
    for bit in bits:
        if bit == 5:
            transfers += [((32, -1), 2), ((32, 1), 3)]
        elif bit == high and (low, high) in ((1, 2), (3, 4)):
            transfers += [(((1 << low) | (1 << high), 0), 4), (((1 << low) | (1 << high), 0), 5)]
        else:
            transfers += [((1 << bit, 0), 0), ((1 << bit, 0), 1)]
    return transfers


def exchange_kernel(transfers, groups, text_ref, image_ref, landed, send_sem, recv_sem):
    blk, group = lax.axis_index("blk"), lax.axis_index("group")
    barrier = pltpu.get_barrier_semaphore()
    moves = []
    for move, _ in transfers:
        for other in (move, (move[0], -move[1])):
            if other not in moves:
                moves.append(other)
    for move in moves:
        pl.semaphore_signal(
            barrier, inc=1, device_id=there(move, blk, group, groups), device_id_type=MESH
        )
    pl.semaphore_wait(barrier, len(moves))
    rows = text_ref.shape[0] // CHUNKS

    def copy(number, chunk):
        move, source = transfers[number]
        span = pl.ds(chunk * rows, rows)
        block = (text_ref, image_ref)[source] if source < 2 else landed.at[source - 2]
        return pltpu.make_async_remote_copy(
            src_ref=block.at[span],
            dst_ref=landed.at[number, span],
            send_sem=send_sem.at[number, chunk],
            recv_sem=recv_sem.at[number, chunk],
            device_id=there(move, blk, group, groups),
            device_id_type=MESH,
        )

    first = [n for n, (_, source) in enumerate(transfers) if source < 2]
    later = [n for n, (_, source) in enumerate(transfers) if source >= 2]
    passed = [transfers[n][1] - 2 for n in later]
    for chunk in range(CHUNKS):
        for number in first:
            copy(number, chunk).start()
    for chunk in range(CHUNKS):
        for number in later:
            copy(transfers[number][1] - 2, chunk).wait_recv()
            copy(number, chunk).start()
    for chunk in range(CHUNKS):
        for number in range(len(transfers)):
            if number not in passed:
                copy(number, chunk).wait_recv()
            copy(number, chunk).wait_send()


def exchange(bits, collective_id, groups, text_half, image_half):
    transfers = plan(bits)
    count = len(transfers)
    return pl.pallas_call(
        functools.partial(exchange_kernel, transfers, groups),
        out_shape=jax.ShapeDtypeStruct((count,) + text_half.shape, jnp.bfloat16),
        in_specs=[pl.BlockSpec(memory_space=pl.ANY)] * 2,
        out_specs=pl.BlockSpec(memory_space=pl.ANY),
        scratch_shapes=[
            pltpu.SemaphoreType.DMA((count, CHUNKS)),
            pltpu.SemaphoreType.DMA((count, CHUNKS)),
        ],
        compiler_params=pltpu.CompilerParams(collective_id=collective_id, has_side_effects=True),
        name="exchange",
    )(text_half, image_half)


def normalize(raw_rows):
    radius = jnp.sqrt(jnp.sum(raw_rows * raw_rows, axis=-1, keepdims=True) + epsilon)
    unit_rows = raw_rows / radius
    return (radius, unit_rows, unit_rows.astype(jnp.bfloat16))


def pair_linkage(left_rows, right_rows, multiplier, offset, matched):
    products = lax.dot_general(
        left_rows, right_rows, (((1,), (1,)), ((), ())), preferred_element_type=jnp.float32
    )
    logits = multiplier * products + offset
    if matched:
        labels = 2.0 * jnp.eye(left_rows.shape[0], dtype=jnp.float32) - 1.0
    else:
        labels = -jnp.ones_like(logits)
    weights = -labels * jax.nn.sigmoid(-labels * logits)
    return (multiplier * weights).astype(jnp.bfloat16)


def toward_left(coupled, right_rows):
    return jnp.dot(coupled, right_rows, preferred_element_type=jnp.float32)


def toward_right(coupled, left_rows):
    return lax.dot_general(
        coupled, left_rows, (((0,), (0,)), ((), ())), preferred_element_type=jnp.float32
    )


def project(radius, unit_rows, gradient):
    radial = jnp.sum(unit_rows * gradient, axis=-1, keepdims=True)
    return (gradient - unit_rows * radial) / radius


def on_device(images, texts, partner_lookup_grid, sharpness_coefficient, sigmoid_shift_term):
    multiplier, offset = sharpness_coefficient[0], sigmoid_shift_term[0]
    groups = lax.axis_size("group")
    bit_count = lax.axis_size("blk").bit_length() - 1
    image_radius, image_unit, image_half = normalize(images)
    text_radius, text_unit, text_half = normalize(texts)
    masks = partner_lookup_grid[:, 0]
    pairs = [(a, b) for a in range(bit_count) for b in range(a + 1, bit_count)]
    wanted = jnp.bitwise_or(masks[0], masks[1])
    branch = sum(
        jnp.where(wanted == (1 << a) + (1 << b), number, 0) for number, (a, b) in enumerate(pairs)
    )
    landed = lax.switch(
        branch,
        [functools.partial(exchange, pair, number, groups) for number, pair in enumerate(pairs)],
        text_half,
        image_half,
    )
    diagonal = pair_linkage(image_half, text_half, multiplier, offset, True)
    image_sum = toward_left(diagonal, text_half)
    text_sum = toward_right(diagonal, image_half)
    for number in range(0, landed.shape[0], 2):
        other_text, other_image = landed[number], landed[number + 1]
        coupled = pair_linkage(image_half, other_text, multiplier, offset, False)
        image_sum = image_sum + toward_left(coupled, other_text)
        coupled = pair_linkage(other_image, text_half, multiplier, offset, False)
        text_sum = text_sum + toward_right(coupled, other_image)
    return (project(image_radius, image_unit, image_sum), project(text_radius, text_unit, text_sum))


def solution(mesh):
    placed = (P(("blk", "group"), None), P(("blk", "group"), None), P(), P(), P())
    return jax.shard_map(
        on_device,
        mesh=mesh,
        in_specs=placed,
        out_specs=(P(("blk", "group"), None), P(("blk", "group"), None)),
        check_vma=False,
    )
```

```python
import functools

import jax
import jax.numpy as jnp
from jax import lax
from jax.experimental import pallas as pl
from jax.experimental.pallas import tpu as pltpu
from jax.sharding import PartitionSpec as P

MESH = pl.DeviceIdType.MESH
epsilon = 1e-06
CHUNKS = 8
TILE = 256
STRIP = 384


def plan(bits):
    low, high = bits
    streams = [((0, 1), None)]
    for bit in bits:
        if bit == 5:
            streams.append(((32, -1), 0))
        elif bit == high and (low, high) in ((1, 2), (3, 4)):
            streams.append((((1 << low) | (1 << high), 0), 1))
        else:
            streams.append(((1 << bit, 0), None))
    return streams


def fused_kernel(
    streams,
    lag,
    groups,
    image_hbm,
    text_hbm,
    multiplier_ref,
    offset_ref,
    image_out,
    text_out,
    raw,
    half,
    inverse,
    landed,
    coupled,
    total,
    load_sem,
    send_sem,
    recv_sem,
    store_sem,
):
    blk, group = lax.axis_index("blk"), lax.axis_index("group")
    rows_all, width = image_hbm.shape
    rows = rows_all // CHUNKS
    sources, results = (image_hbm, text_hbm), (image_out, text_out)

    def there(move):
        return (jnp.bitwise_xor(blk, move[0]), lax.rem(group + move[1] + groups, groups))

    def span(chunk, size=rows):
        return pl.ds(pl.multiple_of(chunk * size, size), size)

    def part(number):
        return pl.ds(number * rows, rows)

    barrier = pltpu.get_barrier_semaphore()
    moves = []
    for move, _ in streams:
        for other in (move, (move[0], -move[1])):
            if other not in moves:
                moves.append(other)
    for move in moves:
        pl.semaphore_signal(barrier, inc=1, device_id=there(move), device_id_type=MESH)

    def load(kind, chunk):
        return pltpu.make_async_copy(
            sources[kind].at[span(chunk)], raw.at[kind, span(chunk)], load_sem.at[kind, chunk]
        )

    def store(kind, chunk):
        return pltpu.make_async_copy(
            total.at[kind, span(chunk)], results[kind].at[span(chunk)], store_sem.at[kind, chunk]
        )

    def copy(kind, number, chunk):
        (mask, step), origin = streams[number]
        return pltpu.make_async_remote_copy(
            src_ref=landed.at[kind, chunk, part(0 if origin is None else origin + 1)],
            dst_ref=landed.at[kind, chunk, part(number + 1)],
            send_sem=send_sem.at[kind, number, chunk],
            recv_sem=recv_sem.at[kind, number, chunk],
            device_id=there((mask, step * (2 * kind - 1))),
            device_id_type=MESH,
        )

    direct = [n for n, (_, origin) in enumerate(streams) if origin is None]
    passing = [n for n, (_, origin) in enumerate(streams) if origin is not None]
    passed = [streams[n][1] for n in passing]

    @pl.loop(0, CHUNKS)
    def _(chunk):
        for kind in (1, 0):
            load(kind, chunk).start()

    @pl.loop(0, CHUNKS)
    def _(chunk):
        for kind in (0, 1):
            total[kind, span(chunk), :] = jnp.zeros((rows, width), jnp.float32)

    pl.semaphore_wait(barrier, len(moves))

    @pl.loop(0, CHUNKS)
    def _(chunk):
        for kind in (1, 0):
            load(kind, chunk).wait()
            x = raw[kind, span(chunk), :]
            scale = 1.0 / jnp.sqrt(jnp.sum(x * x, axis=-1, keepdims=True) + epsilon)
            inverse[kind, span(chunk), :] = scale
            rounded = (x * scale).astype(jnp.bfloat16)
            half[kind, span(chunk), :] = rounded
            landed[kind, chunk, part(0), :] = rounded
            for number in direct:
                copy(kind, number, chunk).start()

    multiplier, offset = multiplier_ref[0], offset_ref[0]

    def absorb(kind, chunk):
        other = landed.at[1 - kind, chunk]

        @pl.loop(0, rows_all // TILE)
        def _(tile):
            products = lax.dot_general(
                half[kind, span(tile, TILE), :],
                other[...],
                (((1,), (1,)), ((), ())),
                preferred_element_type=jnp.float32,
            )
            logits = multiplier * products + offset
            mine = lax.broadcasted_iota(jnp.int32, logits.shape, 0) + tile * TILE
            theirs = lax.broadcasted_iota(jnp.int32, logits.shape, 1)
            theirs = jnp.where(theirs < rows, theirs + chunk * rows, -1)
            same = mine == theirs
            logits = jnp.where(same, -logits, logits)
            weight = jnp.where(same, -multiplier, multiplier)
            coupled[span(tile, TILE), :] = (weight / (1.0 + jnp.exp(-logits))).astype(jnp.bfloat16)

        @pl.loop(0, width // STRIP)
        def _(number):
            strip = span(number, STRIP)
            total[kind, :, strip] += jnp.dot(
                coupled[...], other[:, strip], preferred_element_type=jnp.float32
            )

    @pl.loop(0, CHUNKS + lag)
    def _(turn):
        if passing:

            @pl.when(turn < CHUNKS)
            def _():
                for kind in (1, 0):
                    for number in passing:
                        copy(kind, streams[number][1], turn).wait_recv()
                        copy(kind, number, turn).start()

        @pl.when(turn >= lag)
        def _():
            chunk = turn - lag

            @pl.loop(0, 2)
            def _(kind):
                for number in range(len(streams)):
                    if number not in passed:
                        copy(1 - kind, number, chunk).wait_recv()
                absorb(kind, chunk)

    @pl.loop(0, CHUNKS)
    def _(chunk):
        for kind in (0, 1):
            scale = inverse[kind, span(chunk), :]
            unit = raw[kind, span(chunk), :] * scale
            gradient = total[kind, span(chunk), :]
            radial = jnp.sum(unit * gradient, axis=-1, keepdims=True)
            total[kind, span(chunk), :] = (gradient - unit * radial) * scale
            store(kind, chunk).start()

    @pl.loop(0, CHUNKS)
    def _(chunk):
        for kind in (0, 1):
            store(kind, chunk).wait()
            for number in range(len(streams)):
                copy(kind, number, chunk).wait_send()


def fused(bits, collective_id, groups, images, texts, multiplier, offset):
    streams = plan(bits)
    lag = 0
    if any(origin is not None for _, origin in streams):
        lag = CHUNKS if 5 in bits else 2
    rows, width = images.shape
    count = len(streams)
    return pl.pallas_call(
        functools.partial(fused_kernel, streams, lag, groups),
        out_shape=[jax.ShapeDtypeStruct((rows, width), jnp.float32)] * 2,
        in_specs=[pl.BlockSpec(memory_space=pl.ANY)] * 2
        + [pl.BlockSpec(memory_space=pltpu.SMEM)] * 2,
        out_specs=[pl.BlockSpec(memory_space=pl.ANY)] * 2,
        scratch_shapes=[
            pltpu.VMEM((2, rows, width), jnp.float32),
            pltpu.VMEM((2, rows, width), jnp.bfloat16),
            pltpu.VMEM((2, rows, 1), jnp.float32),
            pltpu.VMEM((2, CHUNKS, (count + 1) * rows // CHUNKS, width), jnp.bfloat16),
            pltpu.VMEM((rows, (count + 1) * rows // CHUNKS), jnp.bfloat16),
            pltpu.VMEM((2, rows, width), jnp.float32),
            pltpu.SemaphoreType.DMA((2, CHUNKS)),
            pltpu.SemaphoreType.DMA((2, count, CHUNKS)),
            pltpu.SemaphoreType.DMA((2, count, CHUNKS)),
            pltpu.SemaphoreType.DMA((2, CHUNKS)),
        ],
        compiler_params=pltpu.CompilerParams(
            collective_id=collective_id, has_side_effects=True, vmem_limit_bytes=48 << 20
        ),
        name="fused",
    )(images, texts, multiplier, offset)


def on_device(images, texts, partner_lookup_grid, sharpness_coefficient, sigmoid_shift_term):
    groups = lax.axis_size("group")
    bit_count = lax.axis_size("blk").bit_length() - 1
    masks = partner_lookup_grid[:, 0]
    pairs = [(a, b) for a in range(bit_count) for b in range(a + 1, bit_count)]
    wanted = jnp.bitwise_or(masks[0], masks[1])
    branch = sum(
        jnp.where(wanted == (1 << a) + (1 << b), number, 0) for number, (a, b) in enumerate(pairs)
    )
    image_gradient, text_gradient = lax.switch(
        branch,
        [functools.partial(fused, pair, number, groups) for number, pair in enumerate(pairs)],
        images,
        texts,
        sharpness_coefficient,
        sigmoid_shift_term,
    )
    return (image_gradient, text_gradient)


def solution(mesh):
    placed = (P(("blk", "group"), None), P(("blk", "group"), None), P(), P(), P())
    return jax.shard_map(
        on_device,
        mesh=mesh,
        in_specs=placed,
        out_specs=(P(("blk", "group"), None), P(("blk", "group"), None)),
        check_vma=False,
    )
```

```python
import functools

import jax
import jax.numpy as jnp
from jax import lax
from jax.experimental import pallas as pl
from jax.experimental.pallas import tpu as pltpu
from jax.sharding import PartitionSpec as P

MESH = pl.DeviceIdType.MESH
epsilon = 1e-06
CHUNKS = 16
MERGE = 1
TILE = 512
STRIP = 384
BLOCK = 64


def plan(bits):
    low, high = bits
    streams = [((0, 1), None)]
    for bit in bits:
        if bit == 5:
            streams.append(((32, -1), 0))
        elif bit == high and (low, high) in ((1, 2), (3, 4)):
            streams.append((((1 << low) | (1 << high), 0), 1))
        else:
            streams.append(((1 << bit, 0), None))
    return streams


def normalize_kernel(grid_ref, image_hbm, text_hbm, half, branch_ref, raw, load_sem):
    pairs = all_pairs(grid_ref.shape[1])
    wanted = jnp.bitwise_or(grid_ref[0, 0], grid_ref[1, 0])
    branch = jnp.int32(0)
    for number, (low, high) in enumerate(pairs):
        branch = jnp.where(wanted == (1 << low) + (1 << high), number, branch)
    branch_ref[0] = branch
    steps = image_hbm.shape[0] // BLOCK

    def load(kind, step):
        place = pl.ds(step * BLOCK, BLOCK)
        source = (image_hbm, text_hbm)[kind]
        return pltpu.make_async_copy(source.at[place], raw.at[kind, place], load_sem.at[kind, step])

    for step in range(steps):
        for kind in (1, 0):
            load(kind, step).start()
    for step in range(steps):
        place = pl.ds(step * BLOCK, BLOCK)
        for kind in (1, 0):
            load(kind, step).wait()
        for kind in (1, 0):
            x = raw[kind, place, :]
            scale = 1.0 / jnp.sqrt(jnp.sum(x * x, axis=-1, keepdims=True) + epsilon)
            half[kind, place, :] = (x * scale).astype(jnp.bfloat16)


def normalize(partner_lookup_grid, images, texts):
    rows, width = images.shape
    return pl.pallas_call(
        normalize_kernel,
        out_shape=[pltpu.VMEM((2, rows, width), jnp.bfloat16), jax.ShapeDtypeStruct((1,), jnp.int32)],
        in_specs=[pl.BlockSpec(memory_space=pltpu.SMEM)] + [pl.BlockSpec(memory_space=pltpu.HBM)] * 2,
        out_specs=[
            pl.BlockSpec(memory_space=pltpu.VMEM),
            pl.BlockSpec(memory_space=pltpu.SMEM),
        ],
        scratch_shapes=[
            pltpu.VMEM((2, rows, width), jnp.float32),
            pltpu.SemaphoreType.DMA((2, rows // BLOCK)),
        ],
        compiler_params=pltpu.CompilerParams(vmem_limit_bytes=56 << 20),
        name="normalize",
    )(partner_lookup_grid, images, texts)


def project_kernel(image_hbm, text_hbm, total, image_out, text_out, raw, load_sem, store_sem):
    steps = image_hbm.shape[0] // BLOCK

    def span(step):
        return pl.ds(pl.multiple_of(step * BLOCK, BLOCK), BLOCK)

    def load(kind, step):
        source = (image_hbm, text_hbm)[kind]
        return pltpu.make_async_copy(
            source.at[span(step)], raw.at[kind, span(step)], load_sem.at[kind, step]
        )

    def store(kind, step):
        result = (image_out, text_out)[kind]
        return pltpu.make_async_copy(
            raw.at[kind, span(step)], result.at[span(step)], store_sem.at[kind, step]
        )

    @pl.loop(0, steps)
    def _(step):
        for kind in (0, 1):
            load(kind, step).start()

    @pl.loop(0, steps)
    def _(step):
        for kind in (0, 1):
            load(kind, step).wait()
        results = []
        for kind in (0, 1):
            x = raw[kind, span(step), :]
            gradient = total[kind, span(step), :]
            scale = 1.0 / jnp.sqrt(jnp.sum(x * x, axis=-1, keepdims=True) + epsilon)
            unit = x * scale
            radial = jnp.sum(unit * gradient, axis=-1, keepdims=True)
            results.append((gradient - unit * radial) * scale)
        for kind in (0, 1):
            raw[kind, span(step), :] = results[kind]
        for kind in (0, 1):
            store(kind, step).start()

    @pl.loop(0, steps)
    def _(step):
        for kind in (0, 1):
            store(kind, step).wait()


def project(images, texts, total):
    rows, width = images.shape
    return pl.pallas_call(
        project_kernel,
        out_shape=[jax.ShapeDtypeStruct((rows, width), jnp.float32)] * 2,
        in_specs=[pl.BlockSpec(memory_space=pl.ANY)] * 2 + [pl.BlockSpec(memory_space=pltpu.VMEM)],
        out_specs=[pl.BlockSpec(memory_space=pl.ANY)] * 2,
        scratch_shapes=[
            pltpu.VMEM((2, rows, width), jnp.float32),
            pltpu.SemaphoreType.DMA((2, rows // BLOCK)),
            pltpu.SemaphoreType.DMA((2, rows // BLOCK)),
        ],
        compiler_params=pltpu.CompilerParams(vmem_limit_bytes=16 << 20),
        name="project",
    )(images, texts, total)


def fused_kernel(
    streams,
    lag,
    window,
    groups,
    half,
    multiplier_ref,
    offset_ref,
    total,
    landed,
    coupled,
    send_sem,
    recv_sem,
):
    blk, group = lax.axis_index("blk"), lax.axis_index("group")
    _, rows_all, width = half.shape
    rows = rows_all // CHUNKS
    block = rows * (len(streams) + 1)

    def there(move):
        return (jnp.bitwise_xor(blk, move[0]), lax.rem(group + move[1] + groups, groups))

    def span(chunk, size=rows):
        return pl.ds(pl.multiple_of(chunk * size, size), size)

    def part(chunk, number):
        return pl.ds(pl.multiple_of(chunk * block + number * rows, rows), rows)

    barrier = pltpu.get_barrier_semaphore()
    moves = []
    for move, _ in streams:
        for other in (move, (move[0], -move[1])):
            if other not in moves:
                moves.append(other)
    for move in moves:
        pl.semaphore_signal(barrier, inc=1, device_id=there(move), device_id_type=MESH)

    def copy(kind, number, chunk):
        (mask, step), origin = streams[number]
        block = half.at[kind, span(chunk)]
        if origin is not None:
            block = landed.at[kind, part(chunk, origin + 1)]
        return pltpu.make_async_remote_copy(
            src_ref=block,
            dst_ref=landed.at[kind, part(chunk, number + 1)],
            send_sem=send_sem.at[kind, number, chunk],
            recv_sem=recv_sem.at[kind, number, chunk],
            device_id=there((mask, step * (2 * kind - 1))),
            device_id_type=MESH,
        )

    direct = [n for n, (_, origin) in enumerate(streams) if origin is None]
    passing = [n for n, (_, origin) in enumerate(streams) if origin is not None]
    passed = [streams[n][1] for n in passing]

    pl.semaphore_wait(barrier, len(moves))

    @pl.loop(0, window)
    def _(chunk):
        for kind in (1, 0):
            for number in direct:
                copy(kind, number, chunk).start()

    @pl.loop(0, CHUNKS)
    def _(chunk):
        for kind in (0, 1):
            landed[kind, part(chunk, 0), :] = half[kind, span(chunk), :]
            total[kind, span(chunk), :] = jnp.zeros((rows, width), jnp.float32)

    multiplier, offset = multiplier_ref[0], offset_ref[0]

    def absorb(unit):
        place = span(unit, MERGE * block)

        @pl.loop(0, rows_all // TILE)
        def _(tile):
            products = [
                lax.dot_general(
                    half[kind, span(tile, TILE), :],
                    landed[1 - kind, place, :],
                    (((1,), (1,)), ((), ())),
                    preferred_element_type=jnp.float32,
                )
                for kind in (0, 1)
            ]
            mine = lax.broadcasted_iota(jnp.int32, products[0].shape, 0) + tile * TILE
            theirs = lax.broadcasted_iota(jnp.int32, products[0].shape, 1)
            same = None
            for sub in range(MERGE):
                first = sub * block
                own = (theirs >= first) & (theirs < first + rows)
                own &= mine == theirs + ((unit * MERGE + sub) * rows - first)
                same = own if same is None else same | own
            weight = jnp.where(same, -multiplier, multiplier)
            for kind in (0, 1):
                logits = multiplier * products[kind] + offset
                logits = jnp.where(same, -logits, logits)
                coupled[kind, span(tile, TILE), :] = (weight / (1.0 + jnp.exp(-logits))).astype(
                    jnp.bfloat16
                )

        @pl.loop(0, width // STRIP)
        def _(number):
            strip = span(number, STRIP)
            for kind in (0, 1):
                total[kind, :, strip] += jnp.dot(
                    coupled[kind], landed[1 - kind, place, strip], preferred_element_type=jnp.float32
                )

    @pl.loop(0, CHUNKS + lag)
    def _(turn):
        if passing:

            @pl.when(turn < CHUNKS)
            def _():
                for kind in (1, 0):
                    for number in passing:
                        copy(kind, streams[number][1], turn).wait_recv()
                        copy(kind, number, turn).start()

        if window < CHUNKS:

            @pl.when(turn < CHUNKS - window)
            def _():
                for kind in (1, 0):
                    for number in direct:
                        copy(kind, number, turn + window).start()

        @pl.when((turn >= lag) & (lax.rem(turn - lag, MERGE) == MERGE - 1))
        def _():
            unit = lax.div(turn - lag, MERGE)
            for kind in (1, 0):
                for sub in range(MERGE):
                    for number in range(len(streams)):
                        if number not in passed:
                            copy(kind, number, unit * MERGE + sub).wait_recv()
            absorb(unit)

    @pl.loop(0, CHUNKS)
    def _(chunk):
        for kind in (0, 1):
            for number in range(len(streams)):
                copy(kind, number, chunk).wait_send()


def fused(bits, collective_id, groups, half, images, texts, multiplier, offset):
    streams = plan(bits)
    lag, window = 0, CHUNKS
    if any(origin is not None for _, origin in streams):
        lag, window = (4, 4) if 5 in bits else (2, CHUNKS)
    _, rows, width = half.shape
    count = len(streams)
    total = pl.pallas_call(
        functools.partial(fused_kernel, streams, lag, window, groups),
        out_shape=pltpu.VMEM((2, rows, width), jnp.float32),
        in_specs=[pl.BlockSpec(memory_space=pltpu.VMEM)]
        + [pl.BlockSpec(memory_space=pltpu.SMEM)] * 2,
        out_specs=pl.BlockSpec(memory_space=pltpu.VMEM),
        scratch_shapes=[
            pltpu.VMEM((2, (count + 1) * rows, width), jnp.bfloat16),
            pltpu.VMEM((2, rows, MERGE * (count + 1) * rows // CHUNKS), jnp.bfloat16),
            pltpu.SemaphoreType.DMA((2, count, CHUNKS)),
            pltpu.SemaphoreType.DMA((2, count, CHUNKS)),
        ],
        compiler_params=pltpu.CompilerParams(
            collective_id=collective_id, has_side_effects=True, vmem_limit_bytes=32 << 20
        ),
        name="fused",
    )(half, multiplier, offset)
    return project(images, texts, total)


def all_pairs(peers):
    bit_count = peers.bit_length() - 1
    return [(a, b) for a in range(bit_count) for b in range(a + 1, bit_count)]


def on_device(images, texts, partner_lookup_grid, sharpness_coefficient, sigmoid_shift_term):
    groups = lax.axis_size("group")
    half, branch = normalize(partner_lookup_grid, images, texts)
    image_gradient, text_gradient = lax.switch(
        branch[0],
        [
            functools.partial(fused, pair, number, groups)
            for number, pair in enumerate(all_pairs(lax.axis_size("blk")))
        ],
        half,
        images,
        texts,
        sharpness_coefficient,
        sigmoid_shift_term,
    )
    return (image_gradient, text_gradient)


def solution(mesh):
    placed = (P(("blk", "group"), None), P(("blk", "group"), None), P(), P(), P())
    return jax.shard_map(
        on_device,
        mesh=mesh,
        in_specs=placed,
        out_specs=(P(("blk", "group"), None), P(("blk", "group"), None)),
        check_vma=False,
    )
```

```python
import functools

import jax
import jax.numpy as jnp
from jax import lax
from jax.experimental import pallas as pl
from jax.experimental.pallas import tpu as pltpu
from jax.sharding import PartitionSpec as P

MESH = pl.DeviceIdType.MESH
epsilon = 1e-06
CHUNKS = 16
MERGE = 1
TILE = 512
STRIP = 384
BLOCK = 64


def plan(bits):
    low, high = bits
    streams = [((0, 1), None)]
    for bit in bits:
        if bit == 5:
            streams.append(((32, -1), 0))
        elif bit == high and (low, high) in ((1, 2), (3, 4)):
            streams.append((((1 << low) | (1 << high), 0), 1))
        else:
            streams.append(((1 << bit, 0), None))
    return streams


def branch_kernel(grid_ref, branch_ref):
    wanted = jnp.bitwise_or(grid_ref[0, 0], grid_ref[1, 0])
    branch = jnp.int32(0)
    for number, (low, high) in enumerate(all_pairs(grid_ref.shape[1])):
        branch = jnp.where(wanted == (1 << low) + (1 << high), number, branch)
    branch_ref[0] = branch


def find_branch(partner_lookup_grid):
    return pl.pallas_call(
        branch_kernel,
        out_shape=jax.ShapeDtypeStruct((1,), jnp.int32),
        in_specs=[pl.BlockSpec(memory_space=pltpu.SMEM)],
        out_specs=pl.BlockSpec(memory_space=pltpu.SMEM),
        name="find_branch",
    )(partner_lookup_grid)[0]


def project_kernel(raw, inverse, total, image_out, text_out, results, store_sem):
    steps = raw.shape[1] // BLOCK

    def span(step):
        return pl.ds(pl.multiple_of(step * BLOCK, BLOCK), BLOCK)

    def store(kind, step):
        return pltpu.make_async_copy(
            results.at[kind, span(step)],
            (image_out, text_out)[kind].at[span(step)],
            store_sem.at[kind, step],
        )

    @pl.loop(0, steps)
    def _(step):
        for kind in (0, 1):
            x, gradient = raw[kind, span(step), :], total[kind, span(step), :]
            scale = inverse[kind, span(step), :]
            radial = scale * (scale * jnp.sum(x * gradient, axis=-1, keepdims=True))
            results[kind, span(step), :] = (gradient - x * radial) * scale
        for kind in (0, 1):
            store(kind, step).start()

    @pl.loop(0, steps)
    def _(step):
        for kind in (0, 1):
            store(kind, step).wait()


def project(raw, inverse, total):
    _, rows, width = raw.shape
    return pl.pallas_call(
        project_kernel,
        out_shape=[jax.ShapeDtypeStruct((rows, width), jnp.float32)] * 2,
        in_specs=[pl.BlockSpec(memory_space=pltpu.VMEM)] * 3,
        out_specs=[pl.BlockSpec(memory_space=pl.ANY)] * 2,
        scratch_shapes=[
            pltpu.VMEM((2, rows, width), jnp.float32),
            pltpu.SemaphoreType.DMA((2, rows // BLOCK)),
        ],
        compiler_params=pltpu.CompilerParams(vmem_limit_bytes=16 << 20),
        name="project",
    )(raw, inverse, total)


def fused_kernel(
    streams,
    lag,
    window,
    groups,
    image_hbm,
    text_hbm,
    multiplier_ref,
    offset_ref,
    total,
    raw,
    inverse,
    half,
    landed,
    coupled,
    load_sem,
    send_sem,
    recv_sem,
):
    blk, group = lax.axis_index("blk"), lax.axis_index("group")
    rows_all, width = image_hbm.shape
    rows = rows_all // CHUNKS
    block = rows * (len(streams) + 1)

    def there(move):
        return (jnp.bitwise_xor(blk, move[0]), lax.rem(group + move[1] + groups, groups))

    def span(chunk, size=rows):
        return pl.ds(pl.multiple_of(chunk * size, size), size)

    def part(chunk, number):
        return pl.ds(pl.multiple_of(chunk * block + number * rows, rows), rows)

    def load(kind, step):
        return pltpu.make_async_copy(
            (image_hbm, text_hbm)[kind].at[span(step, BLOCK)],
            raw.at[kind, span(step, BLOCK)],
            load_sem.at[kind, step],
        )

    @pl.loop(0, rows_all // BLOCK)
    def _(step):
        for kind in (1, 0):
            load(kind, step).start()

    barrier = pltpu.get_barrier_semaphore()
    moves = []
    for move, _ in streams:
        for other in (move, (move[0], -move[1])):
            if other not in moves:
                moves.append(other)
    for move in moves:
        pl.semaphore_signal(barrier, inc=1, device_id=there(move), device_id_type=MESH)

    def copy(kind, number, chunk):
        (mask, step), origin = streams[number]
        block = half.at[kind, span(chunk)]
        if origin is not None:
            block = landed.at[kind, part(chunk, origin + 1)]
        return pltpu.make_async_remote_copy(
            src_ref=block,
            dst_ref=landed.at[kind, part(chunk, number + 1)],
            send_sem=send_sem.at[kind, number, chunk],
            recv_sem=recv_sem.at[kind, number, chunk],
            device_id=there((mask, step * (2 * kind - 1))),
            device_id_type=MESH,
        )

    direct = [n for n, (_, origin) in enumerate(streams) if origin is None]
    passing = [n for n, (_, origin) in enumerate(streams) if origin is not None]
    passed = [streams[n][1] for n in passing]

    pl.semaphore_wait(barrier, len(moves))

    @pl.loop(0, rows_all // BLOCK)
    def _(step):
        place, count = span(step, BLOCK), BLOCK // rows
        for kind in (1, 0):
            load(kind, step).wait()
        for kind in (1, 0):
            x = raw[kind, place, :]
            scale = 1.0 / jnp.sqrt(jnp.sum(x * x, axis=-1, keepdims=True) + epsilon)
            inverse[kind, place, :] = scale
            rounded = (x * scale).astype(jnp.bfloat16)
            half[kind, place, :] = rounded
            for sub in range(count):
                own = part(step * count + sub, 0)
                landed[kind, own, :] = rounded[sub * rows : (sub + 1) * rows]
        for sub in range(count):
            chunk = step * count + sub

            @pl.when(chunk < window)
            def _():
                for kind in (1, 0):
                    for number in direct:
                        copy(kind, number, chunk).start()

    @pl.loop(0, CHUNKS)
    def _(chunk):
        for kind in (0, 1):
            total[kind, span(chunk), :] = jnp.zeros((rows, width), jnp.float32)

    multiplier, offset = multiplier_ref[0], offset_ref[0]

    def absorb(unit):
        place = span(unit, MERGE * block)

        @pl.loop(0, rows_all // TILE)
        def _(tile):
            products = [
                lax.dot_general(
                    half[kind, span(tile, TILE), :],
                    landed[1 - kind, place, :],
                    (((1,), (1,)), ((), ())),
                    preferred_element_type=jnp.float32,
                )
                for kind in (0, 1)
            ]
            mine = lax.broadcasted_iota(jnp.int32, products[0].shape, 0) + tile * TILE
            theirs = lax.broadcasted_iota(jnp.int32, products[0].shape, 1)
            same = None
            for sub in range(MERGE):
                first = sub * block
                own = (theirs >= first) & (theirs < first + rows)
                own &= mine == theirs + ((unit * MERGE + sub) * rows - first)
                same = own if same is None else same | own
            weight = jnp.where(same, -multiplier, multiplier)
            for kind in (0, 1):
                logits = multiplier * products[kind] + offset
                logits = jnp.where(same, -logits, logits)
                coupled[kind, span(tile, TILE), :] = (weight / (1.0 + jnp.exp(-logits))).astype(
                    jnp.bfloat16
                )

        @pl.loop(0, width // STRIP)
        def _(number):
            strip = span(number, STRIP)
            for kind in (0, 1):
                total[kind, :, strip] += jnp.dot(
                    coupled[kind], landed[1 - kind, place, strip], preferred_element_type=jnp.float32
                )

    @pl.loop(0, CHUNKS + lag)
    def _(turn):
        if passing:

            @pl.when(turn < CHUNKS)
            def _():
                for kind in (1, 0):
                    for number in passing:
                        copy(kind, streams[number][1], turn).wait_recv()
                        copy(kind, number, turn).start()

        if window < CHUNKS:

            @pl.when(turn < CHUNKS - window)
            def _():
                for kind in (1, 0):
                    for number in direct:
                        copy(kind, number, turn + window).start()

        @pl.when((turn >= lag) & (lax.rem(turn - lag, MERGE) == MERGE - 1))
        def _():
            unit = lax.div(turn - lag, MERGE)
            for kind in (1, 0):
                for sub in range(MERGE):
                    for number in range(len(streams)):
                        if number not in passed:
                            copy(kind, number, unit * MERGE + sub).wait_recv()
            absorb(unit)

    @pl.loop(0, CHUNKS)
    def _(chunk):
        for kind in (0, 1):
            for number in range(len(streams)):
                copy(kind, number, chunk).wait_send()


def fused(bits, collective_id, groups, images, texts, multiplier, offset):
    streams = plan(bits)
    lag, window = 0, CHUNKS
    if any(origin is not None for _, origin in streams):
        lag, window = (4, 4) if 5 in bits else (2, CHUNKS)
    rows, width = images.shape
    count = len(streams)
    total, raw, inverse = pl.pallas_call(
        functools.partial(fused_kernel, streams, lag, window, groups),
        out_shape=[
            pltpu.VMEM((2, rows, width), jnp.float32),
            pltpu.VMEM((2, rows, width), jnp.float32),
            pltpu.VMEM((2, rows, 1), jnp.float32),
        ],
        in_specs=[pl.BlockSpec(memory_space=pl.ANY)] * 2
        + [pl.BlockSpec(memory_space=pltpu.SMEM)] * 2,
        out_specs=[pl.BlockSpec(memory_space=pltpu.VMEM)] * 3,
        scratch_shapes=[
            pltpu.VMEM((2, rows, width), jnp.bfloat16),
            pltpu.VMEM((2, (count + 1) * rows, width), jnp.bfloat16),
            pltpu.VMEM((2, rows, MERGE * (count + 1) * rows // CHUNKS), jnp.bfloat16),
            pltpu.SemaphoreType.DMA((2, rows // BLOCK)),
            pltpu.SemaphoreType.DMA((2, count, CHUNKS)),
            pltpu.SemaphoreType.DMA((2, count, CHUNKS)),
        ],
        compiler_params=pltpu.CompilerParams(
            collective_id=collective_id, has_side_effects=True, vmem_limit_bytes=50 << 20
        ),
        name="fused",
    )(images, texts, multiplier, offset)
    return project(raw, inverse, total)


def all_pairs(peers):
    bit_count = peers.bit_length() - 1
    return [(a, b) for a in range(bit_count) for b in range(a + 1, bit_count)]


def on_device(images, texts, partner_lookup_grid, sharpness_coefficient, sigmoid_shift_term):
    groups = lax.axis_size("group")
    branch = find_branch(partner_lookup_grid)
    image_gradient, text_gradient = lax.switch(
        branch,
        [
            functools.partial(fused, pair, number, groups)
            for number, pair in enumerate(all_pairs(lax.axis_size("blk")))
        ],
        images,
        texts,
        sharpness_coefficient,
        sigmoid_shift_term,
    )
    return (image_gradient, text_gradient)


def solution(mesh):
    placed = (P(("blk", "group"), None), P(("blk", "group"), None), P(), P(), P())
    return jax.shard_map(
        on_device,
        mesh=mesh,
        in_specs=placed,
        out_specs=(P(("blk", "group"), None), P(("blk", "group"), None)),
        check_vma=False,
    )
```
